512 devices in a mesh: dp: 32 (over y, x), seq: 16 (over z, core).
Axes of the slice: x: 4, y: 8, z: 8, core: 2. Of those that a mesh axis runs over, the one named last changes fastest.
Arguments:
- tokens: bfloat16 [32, 4096, 2048], P('dp', 'seq'), may hold values from -6 to 6
- level_weights: float32 [32, 8, 21, 4096], P('dp', None, None, 'seq'), may hold values from 0.05 to 1
- w_query: bfloat16 [2048, 1024], P('dp'), may hold values from -0.125 to 0.125
- w_key: bfloat16 [2048, 1024], P('dp'), may hold values from -0.125 to 0.125
- w_value: bfloat16 [2048, 1024], P('dp'), may hold values from -0.125 to 0.125
- head_gain: float32 [1024], replicated, may hold values from 0.1 to 1.9
Outputs:
- attended: bfloat16 [32, 4096, 1024], P('dp', 'seq')
The draws below stay inside these ranges and needn't reach their ends.
All inputs are finite; a program needn't handle non-finite values.
Results may differ from the reference program's by a relative error of at most 0.013.
Values may be sent and summed in bfloat16 or wider, within the bound.
No kernel may reach another device: no remote copies, remote signals or barrier semaphores. Data moves between devices by JAX's collectives and lax.ppermute only.
A program may use at most 64 MiB of HBM per device.

```python
import math
import jax
import jax.numpy as jnp
from jax import lax

D = 2048
HEADS = 8
HEAD_DIM = 128
LEVELS = 21
TOK_DEV = 256
DOCS = 32
TOKENS = 4096
N_SEQ = 16


def levels(stream_key, shape, shards, least, top_value):
    def one(axis_at, shards_of):
        draws = jax.random.uniform(jax.random.fold_in(jax.random.fold_in(stream_key, 6), axis_at), (shards_of,), jnp.float32, least / len(shards), top_value / len(shards))
        return jnp.repeat(jnp.exp(draws), shape[axis_at] // shards_of).reshape((-1,) + (1,) * (len(shape) - axis_at - 1))

    factor_of = one(*shards[0])
    for cut in shards[1:]:
        factor_of = factor_of * one(*cut)
    return factor_of


def bell_draw(stream_key, extent, deviation, bound, pieces=(), held_as=jnp.bfloat16):
    array = jax.random.normal(stream_key, extent, jnp.float32) * deviation
    if len(pieces) > 0:
        array = levels(stream_key, extent, pieces, -0.22, 0.18) * array
    return jnp.clip(array, min=-bound, max=bound).astype(held_as)


def setup_inputs(seed: int = 0) -> dict:
    key_of = jax.random.split(jax.random.key(seed), 7)
    tokens = bell_draw(key_of[0], (DOCS, TOKENS, D), 1.0, 6.0, ((0, 32), (1, 16)))
    level_weights = jnp.clip(jnp.exp(math.log(1.0) - 2.9957323 * jax.random.uniform(key_of[1], (DOCS, HEADS, LEVELS, TOKENS), jnp.float32) ** levels(key_of[1], (DOCS, HEADS, LEVELS, TOKENS), ((0, 32), (3, 16)), -0.2, 0.2)), 0.05, 1.0)
    w_query = bell_draw(key_of[2], (D, HEADS * HEAD_DIM), D ** -0.5, 0.125, ((0, 32),))
    w_key = bell_draw(key_of[3], (D, HEADS * HEAD_DIM), D ** -0.5, 0.125, ((0, 32),))
    w_value = bell_draw(key_of[4], (D, HEADS * HEAD_DIM), D ** -0.5, 0.125, ((0, 32),))
    head_gain = jnp.clip(1.0 + 0.18 * jax.random.normal(key_of[5], (HEADS * HEAD_DIM,), jnp.float32), 0.1, 1.9)
    return {"tokens": tokens, "level_weights": level_weights, "w_query": w_query, "w_key": w_key, "w_value": w_value, "head_gain": head_gain}


def level_onehot(length):
    position = jnp.arange(length, dtype=jnp.int32)
    xor_pos = jnp.bitwise_xor(position[:, None], position[None, :])
    level_depth = jnp.zeros((length, length), jnp.int32)
    bit_total = length.bit_length() - 1
    for level_bit in range(bit_total):
        level_depth = level_depth + (jnp.right_shift(xor_pos, level_bit) > 0).astype(jnp.int32)
    causal = position[None, :] <= position[:, None]
    tables = [jnp.where(causal & (level_depth == depth_value), 1.0, 0.0).astype(jnp.float32) for depth_value in range(bit_total + 1)]
    return jnp.stack(tables)

def local_term(queries, keys_all, values_all, weights_here, onehot):
    scores = jnp.einsum('thd,shd->hts', queries, keys_all)
    gating = jnp.einsum('lts,hlt->hts', onehot, weights_here, precision=lax.Precision.HIGHEST)
    mixing = lax.optimization_barrier((gating * scores).astype(jnp.bfloat16)).astype(jnp.float32)
    return jnp.einsum('hts,shd->thd', mixing, values_all)

def reference(tokens, level_weights, w_query, w_key, w_value, head_gain):
    low_bits = TOK_DEV.bit_length() - 1
    seq_bits = N_SEQ.bit_length() - 1
    onehot = level_onehot(TOK_DEV)
    block_ids = jnp.arange(N_SEQ, dtype=jnp.int32)

    def one_document(inputs):
        doc_tokens, doc_weights = inputs
        projected = [jnp.dot(doc_tokens, weight_matrix, preferred_element_type=jnp.float32).astype(jnp.bfloat16) for weight_matrix in (w_query, w_key, w_value)]
        queries, keys_all, values_all = [product.reshape(N_SEQ, TOK_DEV, HEADS, HEAD_DIM).astype(jnp.float32) for product in projected]
        by_block = doc_weights.reshape(HEADS, LEVELS, N_SEQ, TOK_DEV).transpose(2, 0, 1, 3)
        summed = lax.map(lambda block_item: local_term(block_item[0], block_item[1], block_item[2], block_item[3][:, :low_bits + 1, :], onehot), (queries, keys_all, values_all, by_block))
        states = jnp.einsum('rshd,rshe->rhde', keys_all, values_all, precision=lax.Precision.HIGHEST)
        for level_bit in range(seq_bits):
            same_top = jnp.right_shift(block_ids[None, :], level_bit + 1) == jnp.right_shift(block_ids[:, None], level_bit + 1)
            lower_half = jnp.bitwise_and(jnp.right_shift(block_ids[None, :], level_bit), 1) == 0
            upper_half = jnp.bitwise_and(jnp.right_shift(block_ids[:, None], level_bit), 1) == 1
            member = jnp.where(same_top & lower_half & upper_half, 1.0, 0.0).astype(jnp.float32)
            level_sum = jnp.einsum('rp,phde->rhde', member, states, precision=lax.Precision.HIGHEST)
            level_round = lax.optimization_barrier(level_sum.astype(jnp.bfloat16)).astype(jnp.float32)
            remote = jnp.einsum('rthd,rhde->rthe', queries, level_round, precision=lax.Precision.HIGHEST)
            summed = summed + remote * by_block[:, :, low_bits + 1 + level_bit, :].transpose(0, 2, 1)[..., None]
        mean_square = lax.optimization_barrier(jnp.mean(summed * summed, axis=-1, keepdims=True))
        normed = summed * lax.rsqrt(mean_square + 1e-06) * head_gain.reshape(HEADS, HEAD_DIM)
        return normed.reshape(TOKENS, HEADS * HEAD_DIM).astype(jnp.bfloat16)
    return lax.map(one_document, (tokens, level_weights))
```

```python
import jax
import jax.numpy as jnp
from jax import lax
from jax.experimental import pallas as pl
from jax.experimental.pallas import tpu as pltpu
from jax.sharding import Mesh, PartitionSpec as P

HEADS = 8
HEAD_DIM = 128
TOK = 256
LOW_LEVELS = 9
LEVEL_ROWS = 13
PAD_ROWS = 16
GROUP = 4
OWN_HEADS = HEADS // GROUP
OWN_COLS = OWN_HEADS * HEAD_DIM
Y, X = 8, 4
SHARD = 64
F32 = jnp.float32
BF16 = jnp.bfloat16


def dot(a, b, ca, cb):
    return lax.dot_general(a, b, (((ca,), (cb,)), ((), ())), preferred_element_type=F32)


def assemble(x_here, block, whole):
    for here in range(X):

        @pl.when(x_here == here)
        def _():
            for y in range(Y):
                for i in range(X):
                    start = (y * X + (here + i) % X) * SHARD
                    whole[start : start + SHARD, :] = block(y, i)


def kv_kernel(
    place, t0, t1, t2, t3, w0, w1, w2, w3, keys_out, values_out, near_state, pair_state, total, whole
):
    parts = (w0, w1, w2, w3)
    assemble(place[2], lambda y, i: parts[i][y * SHARD : (y + 1) * SHARD, :], whole)
    sums = []
    for j, tokens in enumerate((t0, t1, t2, t3)):
        both = dot(tokens[0:TOK, :], whole[...], 1, 0)
        keys_all = both[:, :OWN_COLS].astype(BF16)
        keys_out[j] = keys_all
        values_all = both[:, OWN_COLS:].T.astype(BF16)
        values_out[j] = values_all
        row = []
        for h in range(OWN_HEADS):
            cols = slice(h * HEAD_DIM, (h + 1) * HEAD_DIM)
            state = dot(values_all[cols], keys_all[:, cols], 1, 0)
            near_state[j, h] = state.astype(BF16)
            row.append(state)
        sums.append(row)
    for h in range(OWN_HEADS):
        low = sums[0][h] + sums[1][h]
        high = sums[2][h] + sums[3][h]
        pair_state[0, h] = low.astype(BF16)
        pair_state[1, h] = high.astype(BF16)
        total[h] = (low + high).astype(BF16)


def gated_quarter(scores, weights, xor_pos, causal, top):
    gate = jnp.broadcast_to(weights[top : top + 1, :], scores.shape)
    for level in range(top - 1, -1, -1):
        gate = jnp.where(xor_pos < 2**level, weights[level : level + 1, :], gate)
    return jnp.where(causal, gate * scores, 0.0).astype(BF16)


def level_weights_of(tokens, head):
    start = pl.multiple_of(head * TOK, TOK)
    return tokens[TOK : TOK + PAD_ROWS, pl.ds(start, TOK)].astype(F32)


def near_kernel(
    place, t0, t1, t2, t3, w, keys_in, values_in, near_state, pair_state, queries_out, part, whole
):
    assemble(place[2], lambda y, i: w[y, i * SHARD : (i + 1) * SHARD, :], whole)
    role = place[0]
    half = TOK // 2
    key_pos = lax.broadcasted_iota(jnp.int32, (half, half), 0)
    query_pos = lax.broadcasted_iota(jnp.int32, (half, half), 1)
    xor_pos = jnp.bitwise_xor(key_pos, query_pos)
    causal = key_pos <= query_pos
    for j, tokens in enumerate((t0, t1, t2, t3)):
        block = jnp.bitwise_xor(role, j)
        use = (
            jnp.bitwise_and(block, 1).astype(F32),
            jnp.right_shift(block, 1).astype(F32),
        )
        queries_all = dot(tokens[0:TOK, :], whole[...], 1, 0).astype(BF16)
        queries_out[j] = queries_all
        for h in range(OWN_HEADS):
            cols = slice(h * HEAD_DIM, (h + 1) * HEAD_DIM)
            queries = queries_all[:, cols]
            keys = keys_in[j, :, cols]
            values = values_in[j, cols, :]
            weights = level_weights_of(tokens, role * OWN_HEADS + h)
            first = dot(keys[:half], queries, 1, 1)
            second = dot(keys[half:], queries[half:], 1, 1)
            mixed_00 = gated_quarter(first[:, :half], weights[:, :half], xor_pos, causal, 7)
            mixed_01 = (first[:, half:] * weights[8:9, half:]).astype(BF16)
            mixed_11 = gated_quarter(second, weights[:, half:], xor_pos, causal, 7)
            near_0 = dot(values[:, :half], mixed_00, 1, 0)
            near_1 = dot(values, jnp.concatenate([mixed_01, mixed_11], 0), 1, 0)
            summed = jnp.concatenate([near_0, near_1], 1)
            states = jnp.concatenate([near_state[j ^ 1, h], pair_state[(j >> 1) ^ 1, h]], 0)
            remote = dot(states, queries, 1, 1)
            for i in range(2):
                row = LOW_LEVELS + i
                summed = summed + remote[i * HEAD_DIM : (i + 1) * HEAD_DIM] * (
                    weights[row : row + 1, :] * use[i]
                )
            part[j, h] = summed


def finish_kernel(place, t0, t1, t2, t3, queries_in, part, far_1, far_2, far_3, gain, out):
    role = place[0]
    group = place[1]
    use = (jnp.bitwise_and(group, 1).astype(F32), jnp.right_shift(group, 1).astype(F32))
    for h in range(OWN_HEADS):
        head = role * OWN_HEADS + h
        cols = slice(h * HEAD_DIM, (h + 1) * HEAD_DIM)
        far_high = (far_2[h].astype(F32) + far_3[h].astype(F32)).astype(BF16)
        states = jnp.concatenate([far_1[h], far_high], 0)
        for j, tokens in enumerate((t0, t1, t2, t3)):
            block = jnp.bitwise_xor(role, j)
            weights = level_weights_of(tokens, head)
            remote = dot(states, queries_in[j, :, cols], 1, 1)
            summed = part[j, h]
            for i in range(2):
                row = LOW_LEVELS + 2 + i
                summed = summed + remote[i * HEAD_DIM : (i + 1) * HEAD_DIM] * (
                    weights[row : row + 1, :] * use[i]
                )
            mean_square = jnp.mean(summed * summed, axis=0, keepdims=True)
            normed = (summed * lax.rsqrt(mean_square + 1e-06)).T * gain[head]
            out[block, :, cols] = normed.astype(BF16)


VMEM = pl.BlockSpec(memory_space=pltpu.VMEM)
SMEM = pl.BlockSpec(memory_space=pltpu.SMEM)


def swap(array, axis, size, bit):
    return lax.ppermute(array, axis, [(i, i ^ bit) for i in range(size)])


def spread_over(array, axis, size):
    return lax.all_to_all(
        jnp.broadcast_to(array[None], (size,) + array.shape), axis, 0, 0, tiled=True
    )


def from_other_x(line):
    return [
        lax.ppermute(line, "x", [((i + shift) % X, i) for i in range(X)]) for shift in range(1, X)
    ]


def call(kernel, name, outs, ins, scratch=(), flops=0):
    return pl.pallas_call(
        kernel,
        out_shape=[jax.ShapeDtypeStruct(shape, dtype) for shape, dtype in outs],
        in_specs=[SMEM if array.dtype == jnp.int32 else VMEM for array in ins],
        out_specs=[VMEM] * len(outs),
        scratch_shapes=list(scratch),
        compiler_params=pltpu.CompilerParams(vmem_limit_bytes=16 * 2**20),
        cost_estimate=pl.CostEstimate(flops=flops, bytes_accessed=8 * 2**20, transcendentals=0),
        name=name,
    )(*ins)


def local(tokens, level_weights, w_query, w_key, w_value, head_gain):
    role = lax.axis_index(("zl", "c"))
    group = lax.axis_index("zh")
    place = jnp.stack([role, group, lax.axis_index("x")]).astype(jnp.int32)
    used = level_weights[0, :, :LEVEL_ROWS, :].astype(BF16)
    rows = used.transpose(1, 0, 2).reshape(LEVEL_ROWS, HEADS * TOK)
    packed = jnp.concatenate([tokens[0], jnp.pad(rows, ((0, PAD_ROWS - LEVEL_ROWS), (0, 0)))], 0)
    from_z = swap(packed, "zl", 2, 1)
    from_c = swap(packed, "c", 2, 1)

    def own(matrix):
        return lax.dynamic_slice_in_dim(matrix, role * OWN_COLS, OWN_COLS, 1)

    kv_line = spread_over(jnp.concatenate([own(w_key), own(w_value)], 1), "y", Y)
    kv_line = kv_line.reshape(Y * SHARD, 2 * OWN_COLS)
    q_here = own(w_query)
    q_row = jnp.concatenate([q_here] + from_other_x(q_here), 0)
    q_row, _ = lax.optimization_barrier((q_row, kv_line))
    q_all = spread_over(q_row, "y", Y)
    kv_other = from_other_x(kv_line)
    kv_kept, _ = lax.optimization_barrier((kv_line, q_all))
    kv_parts = [kv_kept] + kv_other
    from_zc = swap(from_z, "c", 2, 1)
    token_parts = (packed, from_c, from_z, from_zc)
    width = Y * X * SHARD
    state_shape = (OWN_HEADS, HEAD_DIM, HEAD_DIM)
    keys, values, near_state, pair_state, total = call(
        kv_kernel,
        "keys_values",
        [
            ((GROUP, TOK, OWN_COLS), BF16),
            ((GROUP, OWN_COLS, TOK), BF16),
            ((GROUP,) + state_shape, BF16),
            ((2,) + state_shape, BF16),
            (state_shape, BF16),
        ],
        [place, *token_parts, *kv_parts],
        [pltpu.VMEM((width, 2 * OWN_COLS), BF16)],
        2 * GROUP * TOK * width * 2 * OWN_COLS,
    )
    far = [swap(total, "zh", 4, bit) for bit in (1, 2, 3)]
    queries, part = call(
        near_kernel,
        "near",
        [((GROUP, TOK, OWN_COLS), BF16), ((GROUP, OWN_HEADS, HEAD_DIM, TOK), F32)],
        [place, *token_parts, q_all, keys, values, near_state, pair_state],
        [pltpu.VMEM((width, OWN_COLS), BF16)],
        2 * GROUP * TOK * width * OWN_COLS,
    )
    (out,) = call(
        finish_kernel,
        "finish",
        [((GROUP, TOK, OWN_COLS), BF16)],
        [place, *token_parts, queries, part, *far, head_gain.reshape(HEADS, 1, HEAD_DIM)],
        (),
        2 * GROUP * TOK * OWN_COLS * 2 * HEAD_DIM,
    )
    back = lax.all_to_all(out, ("zl", "c"), 0, 0, tiled=True)
    return back.transpose(1, 0, 2).reshape(1, TOK, HEADS * HEAD_DIM)


def solution(mesh):
    fine = Mesh(mesh.devices.reshape(Y, X, 4, 2, 2), ("y", "x", "zh", "zl", "c"))
    dp, seq = ("y", "x"), ("zh", "zl", "c")
    placed = (
        P(dp, seq, None),
        P(dp, None, None, seq),
        P(dp, None),
        P(dp, None),
        P(dp, None),
        P(),
    )
    return jax.shard_map(
        local, mesh=fine, in_specs=placed, out_specs=P(dp, seq, None), check_vma=False
    )
```

```python
import jax
import jax.numpy as jnp
from jax import lax
from jax.experimental import pallas as pl
from jax.experimental.pallas import tpu as pltpu
from jax.sharding import Mesh, PartitionSpec as P

HEADS = 8
HEAD_DIM = 128
TOK = 256
LOW_LEVELS = 9
LEVEL_ROWS = 13
PAD_ROWS = 16
GROUP = 4
OWN_HEADS = HEADS // GROUP
OWN_COLS = OWN_HEADS * HEAD_DIM
Y, X = 8, 4
SHARD = 64
FIRST = 4
CLASS_ROWS = Y * X * SHARD // 4
F32 = jnp.float32
BF16 = jnp.bfloat16


def dot(a, b, ca, cb):
    return lax.dot_general(a, b, (((ca,), (cb,)), ((), ())), preferred_element_type=F32)


def pack_kernel(place, tokens, level_weights, packed):
    for a in range(2):
        for b in range(2):
            apart = 2 * jnp.bitwise_xor(place[2], a) + jnp.bitwise_xor(place[3], b)
            for yh in range(Y // 2):
                pieces = []
                for xh in range(X // 2):
                    start = ((2 * yh + a) * X + 2 * xh) * SHARD
                    pair = tokens[:, start : start + 2 * SHARD]
                    pieces.append(pair[:, b * SHARD : (b + 1) * SHARD])
                to = pl.multiple_of(apart * CLASS_ROWS + yh * (X // 2) * SHARD, 2 * SHARD)
                packed[:TOK, pl.ds(to, 2 * SHARD)] = jnp.concatenate(pieces, 1)
    for h in range(HEADS):
        packed[TOK:, h * TOK : (h + 1) * TOK] = level_weights[:PAD_ROWS, h, :].astype(BF16)


def project_kernel(token_parts, weights, queries_out, keys_out, values_out, state_out):
    rows = jnp.concatenate([w[...] for w in weights], 0)
    states = []
    for j, tokens in enumerate(token_parts):
        every = dot(tokens[0:TOK, :], rows, 1, 0)
        both, queries = every[:, : 2 * OWN_COLS], every[:, 2 * OWN_COLS :]
        queries_out[j] = queries.astype(BF16)
        keys_all = both[:, :OWN_COLS].astype(BF16)
        keys_out[j] = keys_all
        values_all = both[:, OWN_COLS:].T.astype(BF16)
        values_out[j] = values_all
        row = []
        for h in range(OWN_HEADS):
            cols = slice(h * HEAD_DIM, (h + 1) * HEAD_DIM)
            row.append(dot(values_all[cols], keys_all[:, cols], 1, 0))
            state_out[j, h] = row[h].astype(BF16)
        states.append(row)
    return [states[0][h] + states[1][h] for h in range(OWN_HEADS)]


def first_kernel(t0, t1, w0, w1, w2, w3, queries_out, keys_out, values_out, state_out, pair_out, sum_out):
    sums = project_kernel((t0, t1), (w0, w1, w2, w3), queries_out, keys_out, values_out, state_out)
    for h in range(OWN_HEADS):
        pair_out[h] = sums[h].astype(BF16)
        sum_out[h] = sums[h]


def second_kernel(
    t2, t3, w0, w1, w2, w3, sum_in, queries_out, keys_out, values_out, state_out, pair_out, total
):
    sums = project_kernel((t2, t3), (w0, w1, w2, w3), queries_out, keys_out, values_out, state_out)
    for h in range(OWN_HEADS):
        pair_out[h] = sums[h].astype(BF16)
        both = (sums[h] + sum_in[h]).astype(BF16)
        for g in range(4):
            total[g, h] = both


def gated_quarter(scores, weights, xor_pos, causal, top):
    gate = jnp.broadcast_to(weights[top : top + 1, :], scores.shape)
    for level in range(top - 1, -1, -1):
        gate = jnp.where(xor_pos < 2**level, weights[level : level + 1, :], gate)
    return jnp.where(causal, gate * scores, 0.0).astype(BF16)


def attend_kernel(
    place, t0, t1, t2, t3, q0, q1, k0, k1, v0, v1, s0, s1, p0, p1, totals, gain, out, mixed
):
    queries_in, keys_in, values_in, near_state = (q0, q1), (k0, k1), (v0, v1), (s0, s1)
    pair_state = (p0, p1)
    role = place[0]
    group = place[1]
    half = TOK // 2
    key_pos = lax.broadcasted_iota(jnp.int32, (half, half), 0)
    query_pos = lax.broadcasted_iota(jnp.int32, (half, half), 1)
    xor_pos = jnp.bitwise_xor(key_pos, query_pos)
    causal = key_pos <= query_pos
    all_tokens = (t0, t1, t2, t3)

    def weights_of(j, h):
        start = pl.multiple_of((role * OWN_HEADS + h) * TOK, TOK)
        return all_tokens[j][TOK : TOK + PAD_ROWS, pl.ds(start, TOK)].astype(F32)

    for j in range(GROUP):
        for h in range(OWN_HEADS):
            cols = slice(h * HEAD_DIM, (h + 1) * HEAD_DIM)
            queries = queries_in[j >> 1][j & 1, :, cols]
            keys = keys_in[j >> 1][j & 1, :, cols]
            weights = weights_of(j, h)
            first = dot(keys[:half], queries, 1, 1)
            second = dot(keys[half:], queries[half:], 1, 1)
            mixed[j, h, :half, :half] = gated_quarter(first[:, :half], weights[:, :half], xor_pos, causal, 7)
            mixed[j, h, :half, half:] = (first[:, half:] * weights[8:9, half:]).astype(BF16)
            mixed[j, h, half:, half:] = gated_quarter(second, weights[:, half:], xor_pos, causal, 7)

    far_use = (jnp.bitwise_and(group, 1).astype(F32), jnp.right_shift(group, 1).astype(F32))
    for h in range(OWN_HEADS):
        head = role * OWN_HEADS + h
        cols = slice(h * HEAD_DIM, (h + 1) * HEAD_DIM)
        far_low = totals[jnp.bitwise_xor(group, 1), h]
        far_high = (totals[0, h].astype(F32) + totals[1, h].astype(F32)).astype(BF16)
        for j in range(GROUP):
            block = jnp.bitwise_xor(role, j)
            use = (
                jnp.bitwise_and(block, 1).astype(F32),
                jnp.right_shift(block, 1).astype(F32),
            ) + far_use
            weights = weights_of(j, h)
            states = jnp.concatenate(
                [near_state[j >> 1][(j & 1) ^ 1, h], pair_state[(j >> 1) ^ 1][h], far_low, far_high], 0
            )
            remote = dot(states, queries_in[j >> 1][j & 1, :, cols], 1, 1)
            values = values_in[j >> 1][j & 1, cols, :]
            near_0 = dot(values[:, :half], mixed[j, h, :half, :half], 1, 0)
            near_1 = dot(values, mixed[j, h, :, half:], 1, 0)
            summed = jnp.concatenate([near_0, near_1], 1)
            for i in range(4):
                row = LOW_LEVELS + i
                summed = summed + remote[i * HEAD_DIM : (i + 1) * HEAD_DIM] * (
                    weights[row : row + 1, :] * use[i]
                )
            mean_square = jnp.mean(summed * summed, axis=0, keepdims=True)
            normed = (summed * lax.rsqrt(mean_square + 1e-06)).T * gain[head]
            out[block, :, cols] = normed.astype(BF16)


VMEM = pl.BlockSpec(memory_space=pltpu.VMEM)
SMEM = pl.BlockSpec(memory_space=pltpu.SMEM)


def swap(array, axis, size, bit):
    return lax.ppermute(array, axis, [(i, i ^ bit) for i in range(size)])


def spread_over(array, axis, size):
    return lax.all_to_all(
        jnp.broadcast_to(array[None], (size,) + array.shape), axis, 0, 0, tiled=True
    )


def call(kernel, name, outs, ins, scratch=(), flops=0):
    return pl.pallas_call(
        kernel,
        out_shape=[jax.ShapeDtypeStruct(shape, dtype) for shape, dtype in outs],
        in_specs=[SMEM if array.dtype == jnp.int32 else VMEM for array in ins],
        out_specs=[VMEM] * len(outs),
        scratch_shapes=list(scratch),
        compiler_params=pltpu.CompilerParams(vmem_limit_bytes=16 * 2**20),
        cost_estimate=pl.CostEstimate(flops=flops, bytes_accessed=8 * 2**20, transcendentals=0),
        name=name,
    )(*ins)


def local(tokens, level_weights, w_query, w_key, w_value, head_gain):
    role = lax.axis_index(("zl", "c"))
    group = lax.axis_index("zh")
    place = jnp.stack([role, group, lax.axis_index("yl"), lax.axis_index("xl")]).astype(jnp.int32)
    def own(matrix):
        return lax.dynamic_slice_in_dim(matrix, role * OWN_COLS, OWN_COLS, 1)

    columns = jnp.concatenate([own(w_key), own(w_value), own(w_query)], 1)
    columns, tokens_later = lax.optimization_barrier((columns, tokens))
    (packed,) = call(
        pack_kernel,
        "pack",
        [((TOK + PAD_ROWS, Y * X * SHARD), BF16)],
        [place, tokens_later[0], level_weights[0].transpose(1, 0, 2)],
    )
    from_z = swap(packed, "zl", 2, 1)
    from_c = swap(packed, "c", 2, 1)
    same = spread_over(columns, ("yh", "xh"), Y * X // 4).reshape(CLASS_ROWS, 3 * OWN_COLS)
    from_x = lax.ppermute(same, ("xh", "xl"), [(i, (i + 1) % X) for i in range(X)])
    from_y = lax.ppermute(same, ("yh", "yl"), [(i, (i + 1) % Y) for i in range(Y)])
    from_yx = lax.ppermute(
        same,
        ("yh", "yl", "xh", "xl"),
        [(y * X + x, (y - 1) % Y * X + (x - 1) % X) for y in range(Y) for x in range(X)],
    )
    from_zc = swap(from_z, "c", 2, 1)
    token_parts = (packed, from_c, from_z, from_zc)
    weights = (same, from_x, from_y, from_yx)
    state_shape = (OWN_HEADS, HEAD_DIM, HEAD_DIM)
    results = [
        ((2, TOK, OWN_COLS), BF16),
        ((2, TOK, OWN_COLS), BF16),
        ((2, OWN_COLS, TOK), BF16),
        ((2,) + state_shape, BF16),
        (state_shape, BF16),
    ]
    flops = 2 * 2 * TOK * Y * X * SHARD * 3 * OWN_COLS
    *here, sum_here = call(
        first_kernel,
        "project_here",
        results + [(state_shape, F32)],
        [packed, from_c, *weights],
        (),
        FIRST * flops,
    )
    *there, total = call(
        second_kernel,
        "project_there",
        results + [((4,) + state_shape, BF16)],
        [from_z, from_zc, *weights, sum_here],
        (),
        flops,
    )
    totals = lax.all_to_all(total, "zh", 0, 0, tiled=True)
    (out,) = call(
        attend_kernel,
        "attend",
        [((GROUP, TOK, OWN_COLS), BF16)],
        [
            place,
            *token_parts,
            *[array for pair in zip(here, there) for array in pair],
            totals,
            head_gain.reshape(HEADS, 1, HEAD_DIM),
        ],
        [pltpu.VMEM((GROUP, OWN_HEADS, TOK, TOK), BF16)],
    )
    back = lax.all_to_all(out, ("zl", "c"), 0, 0, tiled=True)
    return back.transpose(1, 0, 2).reshape(1, TOK, HEADS * HEAD_DIM)


def solution(mesh):
    fine = Mesh(mesh.devices.reshape(Y // 2, 2, X // 2, 2, 4, 2, 2), ("yh", "yl", "xh", "xl", "zh", "zl", "c"))
    dp, seq = ("yh", "yl", "xh", "xl"), ("zh", "zl", "c")
    placed = (
        P(dp, seq, None),
        P(dp, None, None, seq),
        P(dp, None),
        P(dp, None),
        P(dp, None),
        P(),
    )
    return jax.shard_map(
        local, mesh=fine, in_specs=placed, out_specs=P(dp, seq, None), check_vma=False
    )
```

```python
import jax
import jax.numpy as jnp
from jax import lax
from jax.experimental import pallas as pl
from jax.experimental.pallas import tpu as pltpu
from jax.sharding import Mesh, PartitionSpec as P

HEADS = 8
HEAD_DIM = 128
TOK = 256
LOW_LEVELS = 9
LEVEL_ROWS = 13
PAD_ROWS = 16
GROUP = 4
OWN_HEADS = HEADS // GROUP
OWN_COLS = OWN_HEADS * HEAD_DIM
Y, X = 8, 4
SHARD = 64
FIRST = 4
CLASS_ROWS = Y * X * SHARD // 4
F32 = jnp.float32
BF16 = jnp.bfloat16


def dot(a, b, ca, cb):
    return lax.dot_general(a, b, (((ca,), (cb,)), ((), ())), preferred_element_type=F32)


def pack_kernel(place, tokens, level_weights, packed):
    for a in range(2):
        for b in range(2):
            apart = 2 * jnp.bitwise_xor(place[2], a) + jnp.bitwise_xor(place[3], b)
            for yh in range(Y // 2):
                pieces = []
                for xh in range(X // 2):
                    start = ((2 * yh + a) * X + 2 * xh) * SHARD
                    pair = tokens[:, start : start + 2 * SHARD]
                    pieces.append(pair[:, b * SHARD : (b + 1) * SHARD])
                to = pl.multiple_of(apart * CLASS_ROWS + yh * (X // 2) * SHARD, 2 * SHARD)
                packed[:TOK, pl.ds(to, 2 * SHARD)] = jnp.concatenate(pieces, 1)
    for h in range(HEADS):
        packed[TOK:, h * TOK : (h + 1) * TOK] = level_weights[:PAD_ROWS, h, :].astype(BF16)


def own_class_kernel(t0, t1, t2, w0, part_out, w_out):
    for j, tokens in enumerate((t0, t1, t2)):
        part_out[j] = dot(tokens[0:TOK, :CLASS_ROWS], w0[...], 1, 0)
    w_out[...] = w0[...]


def project_block(j, every, queries_out, keys_out, values_out, state_out):
    both, queries = every[:, : 2 * OWN_COLS], every[:, 2 * OWN_COLS :]
    queries_out[j] = queries.astype(BF16)
    keys_all = both[:, :OWN_COLS].astype(BF16)
    keys_out[j] = keys_all
    values_all = both[:, OWN_COLS:].T.astype(BF16)
    values_out[j] = values_all
    states = []
    for h in range(OWN_HEADS):
        cols = slice(h * HEAD_DIM, (h + 1) * HEAD_DIM)
        state = dot(values_all[cols], keys_all[:, cols], 1, 0)
        state_out[j, h] = state.astype(BF16)
        states.append(state)
    return states


def first_kernel(t0, t1, part, w1, w2, w3, queries_out, keys_out, values_out, state_out, pair_out, sum_out):
    rows = jnp.concatenate([w1[...], w2[...], w3[...]], 0)
    outs = (queries_out, keys_out, values_out, state_out)
    low, high = [
        project_block(j, part[j] + dot(tokens[0:TOK, CLASS_ROWS:], rows, 1, 0), *outs)
        for j, tokens in enumerate((t0, t1))
    ]
    for h in range(OWN_HEADS):
        pair_out[h] = (low[h] + high[h]).astype(BF16)
        sum_out[h] = low[h] + high[h]


def second_kernel(
    t2, t3, part, w0, w1, w2, w3, sum_in, queries_out, keys_out, values_out, state_out, pair_out, total
):
    rows = jnp.concatenate([w1[...], w2[...], w3[...]], 0)
    outs = (queries_out, keys_out, values_out, state_out)
    low = project_block(0, part[2] + dot(t2[0:TOK, CLASS_ROWS:], rows, 1, 0), *outs)
    rows = jnp.concatenate([w0[...], rows], 0)
    high = project_block(1, dot(t3[0:TOK, :], rows, 1, 0), *outs)
    for h in range(OWN_HEADS):
        pair_out[h] = (low[h] + high[h]).astype(BF16)
        both = (low[h] + high[h] + sum_in[h]).astype(BF16)
        for g in range(4):
            total[g, h] = both


def gated_quarter(scores, weights, xor_pos, causal, top):
    gate = jnp.broadcast_to(weights[top : top + 1, :], scores.shape)
    for level in range(top - 1, -1, -1):
        gate = jnp.where(xor_pos < 2**level, weights[level : level + 1, :], gate)
    return jnp.where(causal, gate * scores, 0.0).astype(BF16)


def attend_kernel(
    place, t0, t1, t2, t3, q0, q1, k0, k1, v0, v1, s0, s1, p0, p1, totals, gain, out, mixed
):
    queries_in, keys_in, values_in, near_state = (q0, q1), (k0, k1), (v0, v1), (s0, s1)
    pair_state = (p0, p1)
    role = place[0]
    group = place[1]
    half = TOK // 2
    key_pos = lax.broadcasted_iota(jnp.int32, (half, half), 0)
    query_pos = lax.broadcasted_iota(jnp.int32, (half, half), 1)
    xor_pos = jnp.bitwise_xor(key_pos, query_pos)
    causal = key_pos <= query_pos
    all_tokens = (t0, t1, t2, t3)

    def weights_of(j, h):
        start = pl.multiple_of((role * OWN_HEADS + h) * TOK, TOK)
        return all_tokens[j][:, pl.ds(start, TOK)].astype(F32)

    for j in range(GROUP):
        for h in range(OWN_HEADS):
            cols = slice(h * HEAD_DIM, (h + 1) * HEAD_DIM)
            queries = queries_in[j >> 1][j & 1, :, cols]
            keys = keys_in[j >> 1][j & 1, :, cols]
            weights = weights_of(j, h)
            first = dot(keys[:half], queries, 1, 1)
            second = dot(keys[half:], queries[half:], 1, 1)
            mixed[j, h, :half, :half] = gated_quarter(first[:, :half], weights[:, :half], xor_pos, causal, 7)
            mixed[j, h, :half, half:] = (first[:, half:] * weights[8:9, half:]).astype(BF16)
            mixed[j, h, half:, half:] = gated_quarter(second, weights[:, half:], xor_pos, causal, 7)

    far_use = (jnp.bitwise_and(group, 1).astype(F32), jnp.right_shift(group, 1).astype(F32))
    for h in range(OWN_HEADS):
        head = role * OWN_HEADS + h
        cols = slice(h * HEAD_DIM, (h + 1) * HEAD_DIM)
        far_low = totals[jnp.bitwise_xor(group, 1), h]
        far_high = (totals[0, h].astype(F32) + totals[1, h].astype(F32)).astype(BF16)
        for j in range(GROUP):
            block = jnp.bitwise_xor(role, j)
            use = (
                jnp.bitwise_and(block, 1).astype(F32),
                jnp.right_shift(block, 1).astype(F32),
            ) + far_use
            weights = weights_of(j, h)
            states = jnp.concatenate(
                [near_state[j >> 1][(j & 1) ^ 1, h], pair_state[(j >> 1) ^ 1][h], far_low, far_high], 0
            )
            remote = dot(states, queries_in[j >> 1][j & 1, :, cols], 1, 1)
            values = values_in[j >> 1][j & 1, cols, :]
            near_0 = dot(values[:, :half], mixed[j, h, :half, :half], 1, 0)
            near_1 = dot(values, mixed[j, h, :, half:], 1, 0)
            summed = jnp.concatenate([near_0, near_1], 1)
            for i in range(4):
                row = LOW_LEVELS + i
                summed = summed + remote[i * HEAD_DIM : (i + 1) * HEAD_DIM] * (
                    weights[row : row + 1, :] * use[i]
                )
            mean_square = jnp.mean(summed * summed, axis=0, keepdims=True)
            normed = (summed * lax.rsqrt(mean_square + 1e-06)).T * gain[head]
            out[block, :, cols] = normed.astype(BF16)


VMEM = pl.BlockSpec(memory_space=pltpu.VMEM)
SMEM = pl.BlockSpec(memory_space=pltpu.SMEM)


def swap(array, axis, size, bit):
    return lax.ppermute(array, axis, [(i, i ^ bit) for i in range(size)])


def spread_over(array, axis, size):
    return lax.all_to_all(
        jnp.broadcast_to(array[None], (size,) + array.shape), axis, 0, 0, tiled=True
    )


LEVELS_OF = pl.BlockSpec((PAD_ROWS, Y * X * SHARD), lambda i: (TOK // PAD_ROWS, 0))


def call(kernel, name, outs, ins, scratch=(), flops=0, specs={}):
    return pl.pallas_call(
        kernel,
        out_shape=[jax.ShapeDtypeStruct(shape, dtype) for shape, dtype in outs],
        in_specs=[specs.get(i, SMEM if array.dtype == jnp.int32 else VMEM) for i, array in enumerate(ins)],
        out_specs=[VMEM] * len(outs),
        grid=(1,) if specs else (),
        scratch_shapes=list(scratch),
        compiler_params=pltpu.CompilerParams(vmem_limit_bytes=10 * 2**20),
        cost_estimate=pl.CostEstimate(flops=flops, bytes_accessed=8 * 2**20, transcendentals=0),
        name=name,
    )(*ins)


def local(tokens, level_weights, w_query, w_key, w_value, head_gain):
    role = lax.axis_index(("zl", "c"))
    group = lax.axis_index("zh")
    place = jnp.stack([role, group, lax.axis_index("yl"), lax.axis_index("xl")]).astype(jnp.int32)
    def own(matrix):
        return lax.dynamic_slice_in_dim(matrix, role * OWN_COLS, OWN_COLS, 1)

    columns = jnp.concatenate([own(w_key), own(w_value), own(w_query)], 1)
    columns, tokens_later = lax.optimization_barrier((columns, tokens))
    (packed,) = call(
        pack_kernel,
        "pack",
        [((TOK + PAD_ROWS, Y * X * SHARD), BF16)],
        [place, tokens_later[0], level_weights[0].transpose(1, 0, 2)],
    )
    from_z = swap(packed, "zl", 2, 1)
    from_c = swap(packed, "c", 2, 1)
    same = spread_over(columns, ("yh", "xh"), Y * X // 4).reshape(CLASS_ROWS, 3 * OWN_COLS)
    from_x = lax.ppermute(same, ("xh", "xl"), [(i, (i + 1) % X) for i in range(X)])
    from_y = lax.ppermute(same, ("yh", "yl"), [(i, (i + 1) % Y) for i in range(Y)])
    from_yx = lax.ppermute(
        same,
        ("yh", "yl", "xh", "xl"),
        [(y * X + x, (y - 1) % Y * X + (x - 1) % X) for y in range(Y) for x in range(X)],
    )
    from_zc = swap(from_z, "c", 2, 1)
    token_parts = (packed, from_c, from_z, from_zc)
    columns = 3 * OWN_COLS
    part, same_here = call(
        own_class_kernel,
        "own_class",
        [((3, TOK, columns), F32), ((CLASS_ROWS, columns), BF16)],
        [packed, from_c, from_z, same],
        (),
        2 * 3 * TOK * CLASS_ROWS * columns,
    )
    others = (from_x, from_y, from_yx)
    state_shape = (OWN_HEADS, HEAD_DIM, HEAD_DIM)
    results = [
        ((2, TOK, OWN_COLS), BF16),
        ((2, TOK, OWN_COLS), BF16),
        ((2, OWN_COLS, TOK), BF16),
        ((2,) + state_shape, BF16),
        (state_shape, BF16),
    ]
    flops = 2 * 2 * TOK * Y * X * SHARD * 3 * OWN_COLS
    *here, sum_here = call(
        first_kernel,
        "project_here",
        results + [(state_shape, F32)],
        [packed, from_c, part, *others],
        (),
        FIRST * flops,
    )
    *there, total = call(
        second_kernel,
        "project_there",
        results + [((4,) + state_shape, BF16)],
        [from_z, from_zc, part, same_here, *others, sum_here],
        (),
        flops,
    )
    totals = lax.all_to_all(total, "zh", 0, 0, tiled=True)
    (out,) = call(
        attend_kernel,
        "attend",
        [((GROUP, TOK, OWN_COLS), BF16)],
        [
            place,
            *token_parts,
            *[array for pair in zip(here, there) for array in pair],
            totals,
            head_gain.reshape(HEADS, 1, HEAD_DIM),
        ],
        [pltpu.VMEM((GROUP, OWN_HEADS, TOK, TOK), BF16)],
        specs={i: LEVELS_OF for i in range(1, 1 + GROUP)},
    )
    back = lax.all_to_all(out, ("zl", "c"), 0, 0, tiled=True)
    return back.transpose(1, 0, 2).reshape(1, TOK, HEADS * HEAD_DIM)


def solution(mesh):
    fine = Mesh(mesh.devices.reshape(Y // 2, 2, X // 2, 2, 4, 2, 2), ("yh", "yl", "xh", "xl", "zh", "zl", "c"))
    dp, seq = ("yh", "yl", "xh", "xl"), ("zh", "zl", "c")
    placed = (
        P(dp, seq, None),
        P(dp, None, None, seq),
        P(dp, None),
        P(dp, None),
        P(dp, None),
        P(),
    )
    return jax.shard_map(
        local, mesh=fine, in_specs=placed, out_specs=P(dp, seq, None), check_vma=False
    )
```

```python
import jax
import jax.numpy as jnp
from jax import lax
from jax.experimental import pallas as pl
from jax.experimental.pallas import tpu as pltpu
from jax.sharding import Mesh, PartitionSpec as P

HEADS = 8
HEAD_DIM = 128
TOK = 256
LOW_LEVELS = 9
LEVEL_ROWS = 13
PAD_ROWS = 16
GROUP = 4
OWN_HEADS = HEADS // GROUP
OWN_COLS = OWN_HEADS * HEAD_DIM
Y, X = 8, 4
SHARD = 64
FIRST = 4
CLASS_ROWS = Y * X * SHARD // 4
F32 = jnp.float32
BF16 = jnp.bfloat16


def dot(a, b, ca, cb):
    return lax.dot_general(a, b, (((ca,), (cb,)), ((), ())), preferred_element_type=F32)


def pack_kernel(place, tokens, level_weights, packed):
    for a in range(2):
        for b in range(2):
            apart = 2 * jnp.bitwise_xor(place[2], a) + jnp.bitwise_xor(place[3], b)
            for yh in range(Y // 2):
                pieces = []
                for xh in range(X // 2):
                    start = ((2 * yh + a) * X + 2 * xh) * SHARD
                    pair = tokens[:, start : start + 2 * SHARD]
                    pieces.append(pair[:, b * SHARD : (b + 1) * SHARD])
                to = pl.multiple_of(apart * CLASS_ROWS + yh * (X // 2) * SHARD, 2 * SHARD)
                packed[:TOK, pl.ds(to, 2 * SHARD)] = jnp.concatenate(pieces, 1)
    for h in range(HEADS):
        packed[TOK:, h * TOK : (h + 1) * TOK] = level_weights[:PAD_ROWS, h, :].astype(BF16)


def own_class_kernel(t0, t1, t2, w0, part_out, w_out):
    for j, tokens in enumerate((t0, t1, t2)):
        part_out[j] = dot(tokens[0:TOK, :CLASS_ROWS], w0[...], 1, 0)
    w_out[...] = w0[...]


def two_classes_kernel(t0, t1, t2, part, w2, w3, part_out):
    rows = jnp.concatenate([w2[...], w3[...]], 0)
    for j, tokens in enumerate((t0, t1, t2)):
        part_out[j] = part[j] + dot(tokens[0:TOK, 2 * CLASS_ROWS :], rows, 1, 0)


def project_block(j, every, queries_out, keys_out, values_out, state_out):
    both, queries = every[:, : 2 * OWN_COLS], every[:, 2 * OWN_COLS :]
    queries_out[j] = queries.astype(BF16)
    keys_all = both[:, :OWN_COLS].astype(BF16)
    keys_out[j] = keys_all
    values_all = both[:, OWN_COLS:].T.astype(BF16)
    values_out[j] = values_all
    states = []
    for h in range(OWN_HEADS):
        cols = slice(h * HEAD_DIM, (h + 1) * HEAD_DIM)
        state = dot(values_all[cols], keys_all[:, cols], 1, 0)
        state_out[j, h] = state.astype(BF16)
        states.append(state)
    return states


def first_kernel(t0, t1, part, w1, queries_out, keys_out, values_out, state_out, pair_out, sum_out):
    outs = (queries_out, keys_out, values_out, state_out)
    low, high = [
        project_block(j, part[j] + dot(tokens[0:TOK, CLASS_ROWS : 2 * CLASS_ROWS], w1[...], 1, 0), *outs)
        for j, tokens in enumerate((t0, t1))
    ]
    for h in range(OWN_HEADS):
        pair_out[h] = (low[h] + high[h]).astype(BF16)
        sum_out[h] = low[h] + high[h]


def second_kernel(
    t2, t3, part, w0, w1, w2, w3, sum_in, queries_out, keys_out, values_out, state_out, pair_out, total
):
    outs = (queries_out, keys_out, values_out, state_out)
    low = project_block(0, part[2] + dot(t2[0:TOK, CLASS_ROWS : 2 * CLASS_ROWS], w1[...], 1, 0), *outs)
    rows = jnp.concatenate([w0[...], w1[...], w2[...], w3[...]], 0)
    high = project_block(1, dot(t3[0:TOK, :], rows, 1, 0), *outs)
    for h in range(OWN_HEADS):
        pair_out[h] = (low[h] + high[h]).astype(BF16)
        both = (low[h] + high[h] + sum_in[h]).astype(BF16)
        for g in range(4):
            total[g, h] = both


def gated_quarter(scores, weights, xor_pos, causal, top):
    gate = jnp.broadcast_to(weights[top : top + 1, :], scores.shape)
    for level in range(top - 1, -1, -1):
        gate = jnp.where(xor_pos < 2**level, weights[level : level + 1, :], gate)
    return jnp.where(causal, gate * scores, 0.0).astype(BF16)


def attend_kernel(
    place, t0, t1, t2, t3, q0, q1, k0, k1, v0, v1, s0, s1, p0, p1, totals, gain, out, mixed
):
    queries_in, keys_in, values_in, near_state = (q0, q1), (k0, k1), (v0, v1), (s0, s1)
    pair_state = (p0, p1)
    role = place[0]
    group = place[1]
    half = TOK // 2
    key_pos = lax.broadcasted_iota(jnp.int32, (half, half), 0)
    query_pos = lax.broadcasted_iota(jnp.int32, (half, half), 1)
    xor_pos = jnp.bitwise_xor(key_pos, query_pos)
    causal = key_pos <= query_pos
    all_tokens = (t0, t1, t2, t3)

    def weights_of(j, h):
        start = pl.multiple_of((role * OWN_HEADS + h) * TOK, TOK)
        return all_tokens[j][:, pl.ds(start, TOK)].astype(F32)

    for j in range(GROUP):
        for h in range(OWN_HEADS):
            cols = slice(h * HEAD_DIM, (h + 1) * HEAD_DIM)
            queries = queries_in[j >> 1][j & 1, :, cols]
            keys = keys_in[j >> 1][j & 1, :, cols]
            weights = weights_of(j, h)
            first = dot(keys[:half], queries, 1, 1)
            second = dot(keys[half:], queries[half:], 1, 1)
            mixed[j, h, :half, :half] = gated_quarter(first[:, :half], weights[:, :half], xor_pos, causal, 7)
            mixed[j, h, :half, half:] = (first[:, half:] * weights[8:9, half:]).astype(BF16)
            mixed[j, h, half:, half:] = gated_quarter(second, weights[:, half:], xor_pos, causal, 7)

    far_use = (jnp.bitwise_and(group, 1).astype(F32), jnp.right_shift(group, 1).astype(F32))
    for h in range(OWN_HEADS):
        head = role * OWN_HEADS + h
        cols = slice(h * HEAD_DIM, (h + 1) * HEAD_DIM)
        far_low = totals[jnp.bitwise_xor(group, 1), h]
        far_high = (totals[0, h].astype(F32) + totals[1, h].astype(F32)).astype(BF16)
        for j in range(GROUP):
            block = jnp.bitwise_xor(role, j)
            use = (
                jnp.bitwise_and(block, 1).astype(F32),
                jnp.right_shift(block, 1).astype(F32),
            ) + far_use
            weights = weights_of(j, h)
            states = jnp.concatenate(
                [near_state[j >> 1][(j & 1) ^ 1, h], pair_state[(j >> 1) ^ 1][h], far_low, far_high], 0
            )
            remote = dot(states, queries_in[j >> 1][j & 1, :, cols], 1, 1)
            values = values_in[j >> 1][j & 1, cols, :]
            near_0 = dot(values[:, :half], mixed[j, h, :half, :half], 1, 0)
            near_1 = dot(values, mixed[j, h, :, half:], 1, 0)
            summed = jnp.concatenate([near_0, near_1], 1)
            for i in range(4):
                row = LOW_LEVELS + i
                summed = summed + remote[i * HEAD_DIM : (i + 1) * HEAD_DIM] * (
                    weights[row : row + 1, :] * use[i]
                )
            mean_square = jnp.mean(summed * summed, axis=0, keepdims=True)
            normed = (summed * lax.rsqrt(mean_square + 1e-06)).T * gain[head]
            out[block, :, cols] = normed.astype(BF16)


VMEM = pl.BlockSpec(memory_space=pltpu.VMEM)
SMEM = pl.BlockSpec(memory_space=pltpu.SMEM)


def swap(array, axis, size, bit):
    return lax.ppermute(array, axis, [(i, i ^ bit) for i in range(size)])


def spread_over(array, axis, size):
    return lax.all_to_all(
        jnp.broadcast_to(array[None], (size,) + array.shape), axis, 0, 0, tiled=True
    )


LEVELS_OF = pl.BlockSpec((PAD_ROWS, Y * X * SHARD), lambda i: (TOK // PAD_ROWS, 0))


def call(kernel, name, outs, ins, scratch=(), flops=0, specs={}, traffic=8 * 2**20):
    return pl.pallas_call(
        kernel,
        out_shape=[jax.ShapeDtypeStruct(shape, dtype) for shape, dtype in outs],
        in_specs=[specs.get(i, SMEM if array.dtype == jnp.int32 else VMEM) for i, array in enumerate(ins)],
        out_specs=[VMEM] * len(outs),
        grid=(1,) if specs else (),
        scratch_shapes=list(scratch),
        compiler_params=pltpu.CompilerParams(vmem_limit_bytes=10 * 2**20),
        cost_estimate=pl.CostEstimate(flops=flops, bytes_accessed=traffic, transcendentals=0),
        name=name,
    )(*ins)


def join_kernel(back, out):
    for r in range(GROUP):
        out[:, r * OWN_COLS : (r + 1) * OWN_COLS] = back[r]


def local(tokens, level_weights, w_query, w_key, w_value, head_gain):
    role = lax.axis_index(("zl", "c"))
    group = lax.axis_index("zh")
    place = jnp.stack([role, group, lax.axis_index("yl"), lax.axis_index("xl")]).astype(jnp.int32)
    def own(matrix):
        return lax.dynamic_slice_in_dim(matrix, role * OWN_COLS, OWN_COLS, 1)

    columns = jnp.concatenate([own(w_key), own(w_value), own(w_query)], 1)
    columns, tokens_later = lax.optimization_barrier((columns, tokens))
    (packed,) = call(
        pack_kernel,
        "pack",
        [((TOK + PAD_ROWS, Y * X * SHARD), BF16)],
        [place, tokens_later[0], level_weights[0].transpose(1, 0, 2)],
    )
    from_z = swap(packed, "zl", 2, 1)
    from_c = swap(packed, "c", 2, 1)
    same = spread_over(columns, ("yh", "xh"), Y * X // 4).reshape(CLASS_ROWS, 3 * OWN_COLS)
    from_x = lax.ppermute(same, ("xh", "xl"), [(i, (i + 1) % X) for i in range(X)])
    from_y = lax.ppermute(same, ("yh", "yl"), [(i, (i + 1) % Y) for i in range(Y)])
    from_yx = lax.ppermute(
        same,
        ("yh", "yl", "xh", "xl"),
        [(y * X + x, (y - 1) % Y * X + (x - 1) % X) for y in range(Y) for x in range(X)],
    )
    from_zc = swap(from_z, "c", 2, 1)
    token_parts = (packed, from_c, from_z, from_zc)
    columns = 3 * OWN_COLS
    part, same_here = call(
        own_class_kernel,
        "own_class",
        [((3, TOK, columns), F32), ((CLASS_ROWS, columns), BF16)],
        [packed, from_c, from_z, same],
        (),
        2 * 3 * TOK * CLASS_ROWS * columns,
    )
    others = (from_x, from_y, from_yx)
    (part,) = call(
        two_classes_kernel,
        "two_classes",
        [((3, TOK, columns), F32)],
        [packed, from_c, from_z, part, from_y, from_yx],
        traffic=0,
    )
    state_shape = (OWN_HEADS, HEAD_DIM, HEAD_DIM)
    results = [
        ((2, TOK, OWN_COLS), BF16),
        ((2, TOK, OWN_COLS), BF16),
        ((2, OWN_COLS, TOK), BF16),
        ((2,) + state_shape, BF16),
        (state_shape, BF16),
    ]
    flops = 2 * 2 * TOK * Y * X * SHARD * 3 * OWN_COLS
    *here, sum_here = call(
        first_kernel,
        "project_here",
        results + [(state_shape, F32)],
        [packed, from_c, part, from_x],
        (),
        FIRST * flops,
    )
    *there, total = call(
        second_kernel,
        "project_there",
        results + [((4,) + state_shape, BF16)],
        [from_z, from_zc, part, same_here, *others, sum_here],
        (),
        flops,
    )
    totals = lax.all_to_all(total, "zh", 0, 0, tiled=True)
    (out,) = call(
        attend_kernel,
        "attend",
        [((GROUP, TOK, OWN_COLS), BF16)],
        [
            place,
            *token_parts,
            *[array for pair in zip(here, there) for array in pair],
            totals,
            head_gain.reshape(HEADS, 1, HEAD_DIM),
        ],
        [pltpu.VMEM((GROUP, OWN_HEADS, TOK, TOK), BF16)],
        specs={i: LEVELS_OF for i in range(1, 1 + GROUP)},
    )
    back = lax.all_to_all(out, ("zl", "c"), 0, 0, tiled=True)
    (joined,) = call(join_kernel, "join", [((TOK, HEADS * HEAD_DIM), BF16)], [back])
    return joined[None]


def solution(mesh):
    fine = Mesh(mesh.devices.reshape(Y // 2, 2, X // 2, 2, 4, 2, 2), ("yh", "yl", "xh", "xl", "zh", "zl", "c"))
    dp, seq = ("yh", "yl", "xh", "xl"), ("zh", "zl", "c")
    placed = (
        P(dp, seq, None),
        P(dp, None, None, seq),
        P(dp, None),
        P(dp, None),
        P(dp, None),
        P(),
    )
    return jax.shard_map(
        local, mesh=fine, in_specs=placed, out_specs=P(dp, seq, None), check_vma=False
    )
```

```python
import functools

import jax
import jax.numpy as jnp
from jax import lax
from jax.experimental import pallas as pl
from jax.experimental.pallas import tpu as pltpu
from jax.sharding import Mesh, PartitionSpec as P

HEADS = 8
HEAD_DIM = 128
TOK = 256
LOW_LEVELS = 9
LEVEL_ROWS = 13
PAD_ROWS = 16
GROUP = 4
OWN_HEADS = HEADS // GROUP
OWN_COLS = OWN_HEADS * HEAD_DIM
Y, X = 8, 4
SHARD = 64
FIRST = 4
CLASS_ROWS = Y * X * SHARD // 4
F32 = jnp.float32
BF16 = jnp.bfloat16


def dot(a, b, ca, cb):
    return lax.dot_general(a, b, (((ca,), (cb,)), ((), ())), preferred_element_type=F32)


def pack_kernel(place, tokens, level_weights, packed):
    for a in range(2):
        for b in range(2):
            apart = 2 * jnp.bitwise_xor(place[2], a) + jnp.bitwise_xor(place[3], b)
            for yh in range(Y // 2):
                pieces = []
                for xh in range(X // 2):
                    start = ((2 * yh + a) * X + 2 * xh) * SHARD
                    pair = tokens[:, start : start + 2 * SHARD]
                    pieces.append(pair[:, b * SHARD : (b + 1) * SHARD])
                to = pl.multiple_of(apart * CLASS_ROWS + yh * (X // 2) * SHARD, 2 * SHARD)
                packed[:TOK, pl.ds(to, 2 * SHARD)] = jnp.concatenate(pieces, 1)
    for h in range(HEADS):
        packed[TOK:, h * TOK : (h + 1) * TOK] = level_weights[:PAD_ROWS, h, :].astype(BF16)


def own_class_kernel(t0, t1, t2, w0, part_out, w_out):
    for j, tokens in enumerate((t0, t1, t2)):
        part_out[j] = dot(tokens[0:TOK, :CLASS_ROWS], w0[...], 1, 0)
    w_out[...] = w0[...]


def two_classes_kernel(t0, t1, t2, part, w2, w3, part_out):
    rows = jnp.concatenate([w2[...], w3[...]], 0)
    for j, tokens in enumerate((t0, t1, t2)):
        part_out[j] = part[j] + dot(tokens[0:TOK, 2 * CLASS_ROWS :], rows, 1, 0)


def project_block(j, every, queries_out, keys_out, values_out, state_out):
    both, queries = every[:, : 2 * OWN_COLS], every[:, 2 * OWN_COLS :]
    queries_out[j] = queries.astype(BF16)
    keys_all = both[:, :OWN_COLS].astype(BF16)
    keys_out[j] = keys_all
    values_all = both[:, OWN_COLS:].T.astype(BF16)
    values_out[j] = values_all
    states = []
    for h in range(OWN_HEADS):
        cols = slice(h * HEAD_DIM, (h + 1) * HEAD_DIM)
        state = dot(values_all[cols], keys_all[:, cols], 1, 0)
        state_out[j, h] = state.astype(BF16)
        states.append(state)
    return states


def first_kernel(t0, t1, part, w1, queries_out, keys_out, values_out, state_out, pair_out, sum_out):
    outs = (queries_out, keys_out, values_out, state_out)
    low, high = [
        project_block(j, part[j] + dot(tokens[0:TOK, CLASS_ROWS : 2 * CLASS_ROWS], w1[...], 1, 0), *outs)
        for j, tokens in enumerate((t0, t1))
    ]
    for h in range(OWN_HEADS):
        pair_out[h] = (low[h] + high[h]).astype(BF16)
        sum_out[h] = low[h] + high[h]


def second_kernel(
    t2, t3, part, w0, w1, w2, w3, sum_in, queries_out, keys_out, values_out, state_out, pair_out, total
):
    outs = (queries_out, keys_out, values_out, state_out)
    low = project_block(0, part[2] + dot(t2[0:TOK, CLASS_ROWS : 2 * CLASS_ROWS], w1[...], 1, 0), *outs)
    rows = jnp.concatenate([w0[...], w1[...], w2[...], w3[...]], 0)
    high = project_block(1, dot(t3[0:TOK, :], rows, 1, 0), *outs)
    for h in range(OWN_HEADS):
        pair_out[h] = (low[h] + high[h]).astype(BF16)
        both = (low[h] + high[h] + sum_in[h]).astype(BF16)
        for g in range(4):
            total[g, h] = both


def gated_quarter(scores, weights, xor_pos, causal, top):
    gate = jnp.broadcast_to(weights[top : top + 1, :], scores.shape)
    for level in range(top - 1, -1, -1):
        gate = jnp.where(xor_pos < 2**level, weights[level : level + 1, :], gate)
    return jnp.where(causal, gate * scores, 0.0).astype(BF16)


def attend_kernel(
    pair, ta, tb, q0, q1, k0, k1, v0, v1, s0, s1, p0, p1, totals, gain, out_a, out_b, mixed
):
    queries_in, keys_in, values_in, near_state = (q0, q1), (k0, k1), (v0, v1), (s0, s1)
    pair_state = (p0, p1)
    role = lax.axis_index(("zl", "c"))
    group = lax.axis_index("zh")
    half = TOK // 2
    key_pos = lax.broadcasted_iota(jnp.int32, (half, half), 0)
    query_pos = lax.broadcasted_iota(jnp.int32, (half, half), 1)
    xor_pos = jnp.bitwise_xor(key_pos, query_pos)
    causal = key_pos <= query_pos
    blocks = (2 * pair, 2 * pair + 1)

    def weights_of(j, h):
        start = pl.multiple_of((role * OWN_HEADS + h) * TOK, TOK)
        return (ta, tb)[j & 1][:, pl.ds(start, TOK)].astype(F32)

    for j in blocks:
        for h in range(OWN_HEADS):
            cols = slice(h * HEAD_DIM, (h + 1) * HEAD_DIM)
            queries = queries_in[j >> 1][j & 1, :, cols]
            keys = keys_in[j >> 1][j & 1, :, cols]
            weights = weights_of(j, h)
            first = dot(keys[:half], queries, 1, 1)
            second = dot(keys[half:], queries[half:], 1, 1)
            mixed[j & 1, h, :half, :half] = gated_quarter(first[:, :half], weights[:, :half], xor_pos, causal, 7)
            mixed[j & 1, h, :half, half:] = (first[:, half:] * weights[8:9, half:]).astype(BF16)
            mixed[j & 1, h, half:, half:] = gated_quarter(second, weights[:, half:], xor_pos, causal, 7)

    far_use = (jnp.bitwise_and(group, 1).astype(F32), jnp.right_shift(group, 1).astype(F32))
    for h in range(OWN_HEADS):
        head = role * OWN_HEADS + h
        cols = slice(h * HEAD_DIM, (h + 1) * HEAD_DIM)
        far_low = totals[jnp.bitwise_xor(group, 1), h]
        far_high = (totals[0, h].astype(F32) + totals[1, h].astype(F32)).astype(BF16)
        for j in blocks:
            block = jnp.bitwise_xor(role, j)
            use = (
                jnp.bitwise_and(block, 1).astype(F32),
                jnp.right_shift(block, 1).astype(F32),
            ) + far_use
            weights = weights_of(j, h)
            states = jnp.concatenate(
                [near_state[j >> 1][(j & 1) ^ 1, h], pair_state[(j >> 1) ^ 1][h], far_low, far_high], 0
            )
            remote = dot(states, queries_in[j >> 1][j & 1, :, cols], 1, 1)
            values = values_in[j >> 1][j & 1, cols, :]
            near_0 = dot(values[:, :half], mixed[j & 1, h, :half, :half], 1, 0)
            near_1 = dot(values, mixed[j & 1, h, :, half:], 1, 0)
            summed = jnp.concatenate([near_0, near_1], 1)
            for i in range(4):
                row = LOW_LEVELS + i
                summed = summed + remote[i * HEAD_DIM : (i + 1) * HEAD_DIM] * (
                    weights[row : row + 1, :] * use[i]
                )
            mean_square = jnp.mean(summed * summed, axis=0, keepdims=True)
            normed = (summed * lax.rsqrt(mean_square + 1e-06)).T * gain[head]
            (out_a, out_b)[j & 1][:, cols] = normed.astype(BF16)


VMEM = pl.BlockSpec(memory_space=pltpu.VMEM)
SMEM = pl.BlockSpec(memory_space=pltpu.SMEM)


def swap(array, axis, size, bit):
    return lax.ppermute(array, axis, [(i, i ^ bit) for i in range(size)])


def spread_over(array, axis, size):
    return lax.all_to_all(
        jnp.broadcast_to(array[None], (size,) + array.shape), axis, 0, 0, tiled=True
    )


LEVELS_OF = pl.BlockSpec((PAD_ROWS, Y * X * SHARD), lambda i: (TOK // PAD_ROWS, 0))


def call(kernel, name, outs, ins, scratch=(), flops=0, specs={}, traffic=8 * 2**20):
    return pl.pallas_call(
        kernel,
        out_shape=[jax.ShapeDtypeStruct(shape, dtype) for shape, dtype in outs],
        in_specs=[specs.get(i, SMEM if array.dtype == jnp.int32 else VMEM) for i, array in enumerate(ins)],
        out_specs=[VMEM] * len(outs),
        grid=(1,) if specs else (),
        scratch_shapes=list(scratch),
        compiler_params=pltpu.CompilerParams(vmem_limit_bytes=10 * 2**20),
        cost_estimate=pl.CostEstimate(flops=flops, bytes_accessed=traffic, transcendentals=0),
        name=name,
    )(*ins)


def join_kernel(p0, p1, p2, p3, out):
    role = lax.axis_index(("zl", "c"))
    for j, part in enumerate((p0, p1, p2, p3)):
        start = pl.multiple_of(jnp.bitwise_xor(role, j) * OWN_COLS, OWN_COLS)
        out[:, pl.ds(start, OWN_COLS)] = part[...]


def local(tokens, level_weights, w_query, w_key, w_value, head_gain):
    role = lax.axis_index(("zl", "c"))
    group = lax.axis_index("zh")
    place = jnp.stack([role, group, lax.axis_index("yl"), lax.axis_index("xl")]).astype(jnp.int32)
    def own(matrix):
        return lax.dynamic_slice_in_dim(matrix, role * OWN_COLS, OWN_COLS, 1)

    columns = jnp.concatenate([own(w_key), own(w_value), own(w_query)], 1)
    columns, tokens_later = lax.optimization_barrier((columns, tokens))
    (packed,) = call(
        pack_kernel,
        "pack",
        [((TOK + PAD_ROWS, Y * X * SHARD), BF16)],
        [place, tokens_later[0], level_weights[0].transpose(1, 0, 2)],
    )
    from_z = swap(packed, "zl", 2, 1)
    from_c = swap(packed, "c", 2, 1)
    same = spread_over(columns, ("yh", "xh"), Y * X // 4).reshape(CLASS_ROWS, 3 * OWN_COLS)
    from_x = lax.ppermute(same, ("xh", "xl"), [(i, (i + 1) % X) for i in range(X)])
    from_y = lax.ppermute(same, ("yh", "yl"), [(i, (i + 1) % Y) for i in range(Y)])
    from_yx = lax.ppermute(
        same,
        ("yh", "yl", "xh", "xl"),
        [(y * X + x, (y - 1) % Y * X + (x - 1) % X) for y in range(Y) for x in range(X)],
    )
    from_zc = swap(from_z, "c", 2, 1)
    token_parts = (packed, from_c, from_z, from_zc)
    columns = 3 * OWN_COLS
    part, same_here = call(
        own_class_kernel,
        "own_class",
        [((3, TOK, columns), F32), ((CLASS_ROWS, columns), BF16)],
        [packed, from_c, from_z, same],
        (),
        2 * 3 * TOK * CLASS_ROWS * columns,
    )
    others = (from_x, from_y, from_yx)
    (part,) = call(
        two_classes_kernel,
        "two_classes",
        [((3, TOK, columns), F32)],
        [packed, from_c, from_z, part, from_y, from_yx],
        traffic=0,
    )
    state_shape = (OWN_HEADS, HEAD_DIM, HEAD_DIM)
    results = [
        ((2, TOK, OWN_COLS), BF16),
        ((2, TOK, OWN_COLS), BF16),
        ((2, OWN_COLS, TOK), BF16),
        ((2,) + state_shape, BF16),
        (state_shape, BF16),
    ]
    flops = 2 * 2 * TOK * Y * X * SHARD * 3 * OWN_COLS
    *here, sum_here = call(
        first_kernel,
        "project_here",
        results + [(state_shape, F32)],
        [packed, from_c, part, from_x],
        (),
        FIRST * flops,
    )
    *there, total = call(
        second_kernel,
        "project_there",
        results + [((4,) + state_shape, BF16)],
        [from_z, from_zc, part, same_here, *others, sum_here],
        (),
        flops,
    )
    totals = lax.all_to_all(total, "zh", 0, 0, tiled=True)
    gains = head_gain.reshape(HEADS, 1, HEAD_DIM)
    shared = [array for pair in zip(here, there) for array in pair] + [totals, gains]

    def attend(pair, name):
        return call(
            functools.partial(attend_kernel, pair),
            name,
            [((TOK, OWN_COLS), BF16)] * 2,
            [*token_parts[2 * pair : 2 * pair + 2], *shared],
            [pltpu.VMEM((2, OWN_HEADS, TOK, TOK), BF16)],
            specs={i: LEVELS_OF for i in (0, 1)},
        )

    to_z, to_zc = attend(1, "attend_there")
    kept, to_c = attend(0, "attend_here")
    (joined,) = call(
        join_kernel,
        "join",
        [((TOK, HEADS * HEAD_DIM), BF16)],
        [
            kept,
            swap(to_c, ("zl", "c"), GROUP, 1),
            swap(to_z, ("zl", "c"), GROUP, 2),
            swap(to_zc, ("zl", "c"), GROUP, 3),
        ],
    )
    return joined[None]


def solution(mesh):
    fine = Mesh(mesh.devices.reshape(Y // 2, 2, X // 2, 2, 4, 2, 2), ("yh", "yl", "xh", "xl", "zh", "zl", "c"))
    dp, seq = ("yh", "yl", "xh", "xl"), ("zh", "zl", "c")
    placed = (
        P(dp, seq, None),
        P(dp, None, None, seq),
        P(dp, None),
        P(dp, None),
        P(dp, None),
        P(),
    )
    return jax.shard_map(
        local, mesh=fine, in_specs=placed, out_specs=P(dp, seq, None), check_vma=False
    )
```

```python
import functools

import jax
import jax.numpy as jnp
from jax import lax
from jax.experimental import pallas as pl
from jax.experimental.pallas import tpu as pltpu
from jax.sharding import Mesh, PartitionSpec as P

HEADS = 8
HEAD_DIM = 128
TOK = 256
LOW_LEVELS = 9
LEVEL_ROWS = 13
PAD_ROWS = 16
GROUP = 4
OWN_HEADS = HEADS // GROUP
OWN_COLS = OWN_HEADS * HEAD_DIM
Y, X = 8, 4
SHARD = 64
FIRST = 4
CLASS_ROWS = Y * X * SHARD // 4
F32 = jnp.float32
BF16 = jnp.bfloat16


def dot(a, b, ca, cb):
    return lax.dot_general(a, b, (((ca,), (cb,)), ((), ())), preferred_element_type=F32)


def spread_kernel(w_key, w_value, w_query, out):
    start = pl.multiple_of(lax.axis_index(("zl", "c")) * OWN_COLS, OWN_COLS)
    for i, matrix in enumerate((w_key, w_value, w_query)):
        here = matrix[:, pl.ds(start, OWN_COLS)]
        for copy in range(Y * X // 4):
            out[copy, :, i * OWN_COLS : (i + 1) * OWN_COLS] = here


def pack_kernel(tokens, level_weights, packed):
    for a in range(2):
        for b in range(2):
            apart = 2 * jnp.bitwise_xor(lax.axis_index("yl"), a) + jnp.bitwise_xor(lax.axis_index("xl"), b)
            for yh in range(Y // 2):
                pieces = []
                for xh in range(X // 2):
                    start = ((2 * yh + a) * X + 2 * xh) * SHARD
                    pair = tokens[:, start : start + 2 * SHARD]
                    pieces.append(pair[:, b * SHARD : (b + 1) * SHARD])
                to = pl.multiple_of(apart * CLASS_ROWS + yh * (X // 2) * SHARD, 2 * SHARD)
                packed[:TOK, pl.ds(to, 2 * SHARD)] = jnp.concatenate(pieces, 1)
    for h in range(HEADS):
        packed[TOK:, h * TOK : (h + 1) * TOK] = level_weights[:PAD_ROWS, h, :].astype(BF16)


def own_class_kernel(t0, t1, t2, w0, part_out, w_out):
    for j, tokens in enumerate((t0, t1, t2)):
        part_out[j] = dot(tokens[0:TOK, :CLASS_ROWS], w0[...], 1, 0)
    w_out[...] = w0[...]


def two_classes_kernel(t0, t1, t2, part, w2, w3, part_out):
    rows = jnp.concatenate([w2[...], w3[...]], 0)
    for j, tokens in enumerate((t0, t1, t2)):
        part_out[j] = part[j] + dot(tokens[0:TOK, 2 * CLASS_ROWS :], rows, 1, 0)


def project_block(j, every, queries_out, keys_out, values_out, state_out):
    both, queries = every[:, : 2 * OWN_COLS], every[:, 2 * OWN_COLS :]
    queries_out[j] = queries.astype(BF16)
    keys_all = both[:, :OWN_COLS].astype(BF16)
    keys_out[j] = keys_all
    values_all = both[:, OWN_COLS:].T.astype(BF16)
    values_out[j] = values_all
    states = []
    for h in range(OWN_HEADS):
        cols = slice(h * HEAD_DIM, (h + 1) * HEAD_DIM)
        state = dot(values_all[cols], keys_all[:, cols], 1, 0)
        state_out[j, h] = state.astype(BF16)
        states.append(state)
    return states


def first_kernel(t0, t1, part, w1, queries_out, keys_out, values_out, state_out, pair_out, sum_out):
    outs = (queries_out, keys_out, values_out, state_out)
    low, high = [
        project_block(j, part[j] + dot(tokens[0:TOK, CLASS_ROWS : 2 * CLASS_ROWS], w1[...], 1, 0), *outs)
        for j, tokens in enumerate((t0, t1))
    ]
    for h in range(OWN_HEADS):
        pair_out[h] = (low[h] + high[h]).astype(BF16)
        sum_out[h] = low[h] + high[h]


def second_kernel(
    t2, t3, part, w0, w1, w2, w3, sum_in, queries_out, keys_out, values_out, state_out, pair_out, total
):
    outs = (queries_out, keys_out, values_out, state_out)
    low = project_block(0, part[2] + dot(t2[0:TOK, CLASS_ROWS : 2 * CLASS_ROWS], w1[...], 1, 0), *outs)
    rows = jnp.concatenate([w0[...], w1[...], w2[...], w3[...]], 0)
    high = project_block(1, dot(t3[0:TOK, :], rows, 1, 0), *outs)
    for h in range(OWN_HEADS):
        pair_out[h] = (low[h] + high[h]).astype(BF16)
        both = (low[h] + high[h] + sum_in[h]).astype(BF16)
        for g in range(4):
            total[g, h] = both


def gated_quarter(scores, weights, xor_pos, causal, top):
    gate = jnp.broadcast_to(weights[top : top + 1, :], scores.shape)
    for level in range(top - 1, -1, -1):
        gate = jnp.where(xor_pos < 2**level, weights[level : level + 1, :], gate)
    return jnp.where(causal, gate * scores, 0.0).astype(BF16)


def attend_kernel(
    pair, ta, tb, q0, q1, k0, k1, v0, v1, s0, s1, p0, p1, totals, gain, out_a, out_b, mixed
):
    queries_in, keys_in, values_in, near_state = (q0, q1), (k0, k1), (v0, v1), (s0, s1)
    pair_state = (p0, p1)
    role = lax.axis_index(("zl", "c"))
    group = lax.axis_index("zh")
    half = TOK // 2
    key_pos = lax.broadcasted_iota(jnp.int32, (half, half), 0)
    query_pos = lax.broadcasted_iota(jnp.int32, (half, half), 1)
    xor_pos = jnp.bitwise_xor(key_pos, query_pos)
    causal = key_pos <= query_pos
    blocks = (2 * pair, 2 * pair + 1)

    def weights_of(j, h):
        start = pl.multiple_of((role * OWN_HEADS + h) * TOK, TOK)
        return (ta, tb)[j & 1][:, pl.ds(start, TOK)].astype(F32)

    for j in blocks:
        for h in range(OWN_HEADS):
            cols = slice(h * HEAD_DIM, (h + 1) * HEAD_DIM)
            queries = queries_in[j >> 1][j & 1, :, cols]
            keys = keys_in[j >> 1][j & 1, :, cols]
            weights = weights_of(j, h)
            first = dot(keys[:half], queries, 1, 1)
            second = dot(keys[half:], queries[half:], 1, 1)
            mixed[j & 1, h, :half, :half] = gated_quarter(first[:, :half], weights[:, :half], xor_pos, causal, 7)
            mixed[j & 1, h, :half, half:] = (first[:, half:] * weights[8:9, half:]).astype(BF16)
            mixed[j & 1, h, half:, half:] = gated_quarter(second, weights[:, half:], xor_pos, causal, 7)

    far_use = (jnp.bitwise_and(group, 1).astype(F32), jnp.right_shift(group, 1).astype(F32))
    for h in range(OWN_HEADS):
        head = role * OWN_HEADS + h
        cols = slice(h * HEAD_DIM, (h + 1) * HEAD_DIM)
        far_low = totals[jnp.bitwise_xor(group, 1), h]
        far_high = (totals[0, h].astype(F32) + totals[1, h].astype(F32)).astype(BF16)
        for j in blocks:
            block = jnp.bitwise_xor(role, j)
            use = (
                jnp.bitwise_and(block, 1).astype(F32),
                jnp.right_shift(block, 1).astype(F32),
            ) + far_use
            weights = weights_of(j, h)
            states = jnp.concatenate(
                [near_state[j >> 1][(j & 1) ^ 1, h], pair_state[(j >> 1) ^ 1][h], far_low, far_high], 0
            )
            remote = dot(states, queries_in[j >> 1][j & 1, :, cols], 1, 1)
            values = values_in[j >> 1][j & 1, cols, :]
            near_0 = dot(values[:, :half], mixed[j & 1, h, :half, :half], 1, 0)
            near_1 = dot(values, mixed[j & 1, h, :, half:], 1, 0)
            summed = jnp.concatenate([near_0, near_1], 1)
            for i in range(4):
                row = LOW_LEVELS + i
                summed = summed + remote[i * HEAD_DIM : (i + 1) * HEAD_DIM] * (
                    weights[row : row + 1, :] * use[i]
                )
            mean_square = jnp.mean(summed * summed, axis=0, keepdims=True)
            normed = (summed * lax.rsqrt(mean_square + 1e-06)).T * gain[head]
            (out_a, out_b)[j & 1][:, cols] = normed.astype(BF16)


VMEM = pl.BlockSpec(memory_space=pltpu.VMEM)
SMEM = pl.BlockSpec(memory_space=pltpu.SMEM)


def swap(array, axis, size, bit):
    return lax.ppermute(array, axis, [(i, i ^ bit) for i in range(size)])


LEVELS_OF = pl.BlockSpec((PAD_ROWS, Y * X * SHARD), lambda i: (TOK // PAD_ROWS, 0))


def call(kernel, name, outs, ins, scratch=(), flops=0, specs={}, traffic=8 * 2**20):
    return pl.pallas_call(
        kernel,
        out_shape=[jax.ShapeDtypeStruct(shape, dtype) for shape, dtype in outs],
        in_specs=[specs.get(i, SMEM if array.dtype == jnp.int32 else VMEM) for i, array in enumerate(ins)],
        out_specs=[VMEM] * len(outs),
        grid=(1,) if specs else (),
        scratch_shapes=list(scratch),
        compiler_params=pltpu.CompilerParams(vmem_limit_bytes=10 * 2**20),
        cost_estimate=pl.CostEstimate(flops=flops, bytes_accessed=traffic, transcendentals=0),
        name=name,
    )(*ins)


def join_kernel(p0, p1, p2, p3, out):
    role = lax.axis_index(("zl", "c"))
    for j, part in enumerate((p0, p1, p2, p3)):
        start = pl.multiple_of(jnp.bitwise_xor(role, j) * OWN_COLS, OWN_COLS)
        out[:, pl.ds(start, OWN_COLS)] = part[...]


def local(tokens, level_weights, w_query, w_key, w_value, head_gain):
    (spread,) = call(
        spread_kernel,
        "spread",
        [((Y * X // 4, SHARD, 3 * OWN_COLS), BF16)],
        [w_key, w_value, w_query],
        traffic=0,
    )
    spread, tokens_later = lax.optimization_barrier((spread, tokens))
    (packed,) = call(
        pack_kernel,
        "pack",
        [((TOK + PAD_ROWS, Y * X * SHARD), BF16)],
        [tokens_later[0], level_weights[0].transpose(1, 0, 2)],
    )
    from_z = swap(packed, "zl", 2, 1)
    from_c = swap(packed, "c", 2, 1)
    same = lax.all_to_all(spread, ("yh", "xh"), 0, 0, tiled=True).reshape(CLASS_ROWS, 3 * OWN_COLS)
    from_x = lax.ppermute(same, ("xh", "xl"), [(i, (i + 1) % X) for i in range(X)])
    from_y = lax.ppermute(same, ("yh", "yl"), [(i, (i + 1) % Y) for i in range(Y)])
    from_yx = lax.ppermute(
        same,
        ("yh", "yl", "xh", "xl"),
        [(y * X + x, (y - 1) % Y * X + (x - 1) % X) for y in range(Y) for x in range(X)],
    )
    from_zc = swap(from_z, "c", 2, 1)
    token_parts = (packed, from_c, from_z, from_zc)
    columns = 3 * OWN_COLS
    part, same_here = call(
        own_class_kernel,
        "own_class",
        [((3, TOK, columns), F32), ((CLASS_ROWS, columns), BF16)],
        [packed, from_c, from_z, same],
        (),
        2 * 3 * TOK * CLASS_ROWS * columns,
    )
    others = (from_x, from_y, from_yx)
    (part,) = call(
        two_classes_kernel,
        "two_classes",
        [((3, TOK, columns), F32)],
        [packed, from_c, from_z, part, from_y, from_yx],
        traffic=0,
    )
    state_shape = (OWN_HEADS, HEAD_DIM, HEAD_DIM)
    results = [
        ((2, TOK, OWN_COLS), BF16),
        ((2, TOK, OWN_COLS), BF16),
        ((2, OWN_COLS, TOK), BF16),
        ((2,) + state_shape, BF16),
        (state_shape, BF16),
    ]
    flops = 2 * 2 * TOK * Y * X * SHARD * 3 * OWN_COLS
    *here, sum_here = call(
        first_kernel,
        "project_here",
        results + [(state_shape, F32)],
        [packed, from_c, part, from_x],
        (),
        FIRST * flops,
    )
    *there, total = call(
        second_kernel,
        "project_there",
        results + [((4,) + state_shape, BF16)],
        [from_z, from_zc, part, same_here, *others, sum_here],
        (),
        flops,
    )
    totals = lax.all_to_all(total, "zh", 0, 0, tiled=True)
    gains = head_gain.reshape(HEADS, 1, HEAD_DIM)
    shared = [array for pair in zip(here, there) for array in pair] + [totals, gains]

    def attend(pair, name):
        return call(
            functools.partial(attend_kernel, pair),
            name,
            [((TOK, OWN_COLS), BF16)] * 2,
            [*token_parts[2 * pair : 2 * pair + 2], *shared],
            [pltpu.VMEM((2, OWN_HEADS, TOK, TOK), BF16)],
            specs={i: LEVELS_OF for i in (0, 1)},
        )

    to_z, to_zc = attend(1, "attend_there")
    kept, to_c = attend(0, "attend_here")
    (joined,) = call(
        join_kernel,
        "join",
        [((TOK, HEADS * HEAD_DIM), BF16)],
        [
            kept,
            swap(to_c, ("zl", "c"), GROUP, 1),
            swap(to_z, ("zl", "c"), GROUP, 2),
            swap(to_zc, ("zl", "c"), GROUP, 3),
        ],
    )
    return joined[None]


def solution(mesh):
    fine = Mesh(mesh.devices.reshape(Y // 2, 2, X // 2, 2, 4, 2, 2), ("yh", "yl", "xh", "xl", "zh", "zl", "c"))
    dp, seq = ("yh", "yl", "xh", "xl"), ("zh", "zl", "c")
    placed = (
        P(dp, seq, None),
        P(dp, None, None, seq),
        P(dp, None),
        P(dp, None),
        P(dp, None),
        P(),
    )
    return jax.shard_map(
        local, mesh=fine, in_specs=placed, out_specs=P(dp, seq, None), check_vma=False
    )
```
